512 devices in a mesh: txt: 16 (over y_hi, z), aud: 32 (over x, y_lo, core).
Axes of the slice: x: 4, y: 8 (y_hi: 2, y_lo: 4; y = y_hi * 4 + y_lo), z: 8, core: 2. Of those that a mesh axis runs over, the one named last changes fastest.
Arguments:
- images: float32 [131072, 1024], P(('txt', 'aud')), may hold values from -2 to 2
- texts: float32 [256, 1024], P('txt'), may hold values from -2 to 2
- audio: float32 [128, 1024], P('aud'), may hold values from -2 to 2
- pos_text: int32 [131072], P(('txt', 'aud')), may hold values from 0 to 255
- pos_audio: int32 [131072], P(('txt', 'aud')), may hold values from 0 to 11
- logit_scale: float32 [1], replicated, may hold values from 1 to 4
- logit_bias: float32 [1], replicated, may hold values from -3 to -1
Outputs:
- grad_images: float32 [131072, 1024], P(('txt', 'aud'))
- grad_texts: float32 [256, 1024], P('txt')
- grad_audio: float32 [128, 1024], P('aud')
The draws below stay inside these ranges and needn't reach their ends.
All inputs are finite; a program needn't handle non-finite values.
Results may differ from the reference program's by a relative error of at most 0.0044.
Values sent between devices are 32-bit elements; how exact they have to be, the bound alone decides.
No kernel may reach another device: no remote copies, remote signals or barrier semaphores. Data moves between devices by JAX's collectives and lax.ppermute only.
A program may use at most 64 MiB of HBM per device.

```python
import math
import jax
import jax.numpy as jnp
from jax import lax

D = 1024
I_DEV = 256
AB = 4
HOPS = 2
IMAGES = 131072
TEXTS = 256
AUDIO = 128
N_TXT = 16
N_AUD = 32


def set_ends(result, rng, least, high):
    dims = result.shape
    spot = [jax.random.randint(jax.random.fold_in(rng, axis), (), 0, dims[axis]) for axis in range(len(dims))]
    result = result.at[tuple(spot)].set(least)
    longest = dims.index(max(dims))
    spot[longest] = (spot[longest] + 1) % dims[longest]
    return result.at[tuple(spot)].set(high)


def levels(rng, dims, shards, low, top_value):
    factor_of, own = 1.0, jax.random.fold_in(rng, 6)
    for dim, shards_of in shards:
        heights = jnp.exp(jax.random.uniform(jax.random.fold_in(own, dim), (shards_of,), jnp.float32, low / len(shards), top_value / len(shards)))
        factor_of = factor_of * jnp.repeat(heights, dims[dim] // shards_of).reshape([-1 if axis == dim else 1 for axis in range(len(dims))])
    return factor_of


def scatter_about(own_key, dims, deviation, reach, shards=(), kind=jnp.bfloat16):
    array = deviation * jax.random.normal(own_key, dims, jnp.float32)
    if shards:
        array = array * levels(own_key, dims, shards, -0.22, 0.18)
    return jnp.clip(array, -reach, reach).astype(kind)


def setup_inputs(seed: int = 0) -> dict:
    key_list = jax.random.split(jax.random.key(seed), 8)
    return {
        "images": scatter_about(key_list[0], (IMAGES, D), 0.3, 2.0, ((0, 512),), jnp.float32),
        "texts": scatter_about(key_list[1], (TEXTS, D), 0.3, 2.0, ((0, 16),), jnp.float32),
        "audio": scatter_about(key_list[2], (AUDIO, D), 0.3, 2.0, ((0, 32),), jnp.float32),
        "pos_text": set_ends(jax.random.randint(key_list[3], (IMAGES,), 0, TEXTS), jax.random.fold_in(key_list[3], 1), 0, TEXTS - 1).astype(jnp.int32),
        "pos_audio": set_ends(jax.random.randint(key_list[4], (IMAGES,), 0, (HOPS + 1) * AB), jax.random.fold_in(key_list[4], 1), 0, ((HOPS + 1) * AB) - 1).astype(jnp.int32),
        "logit_scale": jnp.clip(jnp.exp(jax.random.uniform(key_list[5], (1,), jnp.float32, math.log(1.0), math.log(4.0))), 1.0, 4.0),
        "logit_bias": jnp.clip(jax.random.uniform(key_list[6], (1,), jnp.float32, -3.0, -1.0), -3.0, -1.0),
    }


def block_terms(image_half, text_piece, window, first_row, pos_text, pos_audio, temper, offset):
    row_count = text_piece.shape[0]
    slot_count = window.shape[0]
    products = (text_piece[:, None, :] * window[None, :, :]).reshape(row_count * slot_count, -1).astype(jnp.bfloat16)
    logits = temper * lax.dot_general(image_half, products, (((1,), (1,)), ((), ())), preferred_element_type=jnp.float32) + offset
    columns = jnp.arange(row_count * slot_count, dtype=jnp.int32)
    text_of = first_row + columns // slot_count
    slot_of = columns % slot_count
    positive = (text_of[None, :] == pos_text[:, None]) & (slot_of[None, :] == pos_audio[:, None])
    slope = ((jax.nn.sigmoid(logits) - positive.astype(jnp.float32)) * temper).astype(jnp.bfloat16)
    grad_image = jnp.dot(slope, products, preferred_element_type=jnp.float32)
    grad_prod = lax.dot_general(slope, image_half, (((0,), (0,)), ((), ())), preferred_element_type=jnp.float32)
    grad_prod = grad_prod.reshape(row_count, slot_count, -1)
    grad_piece = jnp.sum(grad_prod * window[None, :, :], axis=1)
    grad_window = jnp.sum(grad_prod * text_piece[:, None, :], axis=0)
    return grad_image, grad_piece, grad_window


def reference(images, texts, audio, pos_text, pos_audio, logit_scale, logit_bias):
    temper = logit_scale[0]
    offset = logit_bias[0]
    audio_blocks = audio.reshape(N_AUD, AB, D)

    def visit(carry, block):
        text_acc, audio_acc = carry
        column = block % N_AUD
        picks = ((column + jnp.arange(HOPS + 1, dtype=jnp.int32)) % N_AUD).astype(jnp.int32)
        window = jnp.take(audio_blocks, picks, axis=0).reshape((HOPS + 1) * AB, D)
        first = (block * I_DEV).astype(jnp.int32)
        image_rows = lax.dynamic_slice_in_dim(images, first, I_DEV, 0)
        text_pos = lax.dynamic_slice_in_dim(pos_text, first, I_DEV, 0)
        audio_pos = lax.dynamic_slice_in_dim(pos_audio, first, I_DEV, 0)
        grad_image, grad_piece, grad_window = block_terms(image_rows.astype(jnp.bfloat16), texts, window, jnp.int32(0), text_pos, audio_pos, temper, offset)
        audio_acc = audio_acc.at[picks].add(grad_window.reshape(HOPS + 1, AB, D))
        return (text_acc + grad_piece, audio_acc), grad_image

    start_state = (jnp.zeros((TEXTS, D), jnp.float32), jnp.zeros((N_AUD, AB, D), jnp.float32))
    blocks = jnp.arange(N_TXT * N_AUD, dtype=jnp.int32)
    (grad_texts, grad_audio), grad_images = lax.scan(visit, start_state, blocks)
    return grad_images.reshape(IMAGES, D), grad_texts, grad_audio.reshape(AUDIO, D)
```

```python
import jax
import jax.numpy as jnp
from jax import lax
from jax.experimental import pallas as pl
from jax.experimental.pallas import tpu as pltpu
from jax.sharding import PartitionSpec as P

BOTH = ("txt", "aud")
N_TXT, N_AUD = 16, 32
F32, BF16 = jnp.float32, jnp.bfloat16
VMEM = pl.BlockSpec(memory_space=pltpu.VMEM)
SMEM = pl.BlockSpec(memory_space=pltpu.SMEM)
PARAMS = pltpu.CompilerParams(vmem_limit_bytes=56 * 1024 * 1024)


def device(high, z, x, low, core):
    return (high * 8 + z) * N_AUD + (x * 4 + low) * 2 + core


def groups_by(key):
    found = {}
    for high in range(2):
        for z in range(8):
            for x in range(4):
                for low in range(4):
                    for core in range(2):
                        place = (high, z, x, low, core)
                        found.setdefault(key(*place), []).append(device(*place))
    return [found[k] for k in sorted(found)]


TEXT_GROUPS = groups_by(lambda high, z, x, low, core: (x, low if high == 0 else low ^ 2, core))
CHIP_GROUPS = groups_by(lambda high, z, x, low, core: (high, z, core))

OTHER_CORE = [(i, i ^ 1) for i in range(N_AUD)]
FROM_NEXT = [(i, (i - 2) % N_AUD) for i in range(N_AUD)]
FROM_NEXT_OTHER = [(i, ((i - 2) % N_AUD) ^ 1) for i in range(N_AUD)]
TO_NEXT = [(i, (i + 2) % N_AUD) for i in range(N_AUD)]


def prepare_kernel(core_ref, own_ref, other_ref, own_audio, far_audio, next_own, next_far, half_ref, window_ref):
    core = core_ref[0]
    half_ref[pl.ds(pl.multiple_of(core * 256, 256), 256), :] = own_ref[...].astype(BF16)
    half_ref[pl.ds(pl.multiple_of((1 - core) * 256, 256), 256), :] = other_ref[...].astype(BF16)
    first = core == 0
    a, b = own_audio[...], far_audio[0:4, :]
    window_ref[0:4, :] = jnp.where(first, a, b)
    window_ref[4:8, :] = jnp.where(first, b, a)
    a, b = next_own[...], next_far[...]
    window_ref[8:12, :] = jnp.where(first, a, b)
    window_ref[12:16, :] = jnp.where(first, b, a)


BLOCK_COLUMNS = ((0, 256), (0, 512), (0, 512), (256, 512))


def slope_kernel(
    core_ref, scalar_ref, texts, half_ref, window_ref, own_pos, other_pos,
    slope_ref, text_ref, keep_ref, send_ref, products, audio_sum,
):
    core = core_ref[0]
    temper, offset = scalar_ref[0], scalar_ref[1]
    own, other = own_pos[...], other_pos[...]
    positions = jnp.where(
        core == 0,
        jnp.concatenate([own, other], axis=1),
        jnp.concatenate([other, own], axis=1),
    )
    text_pos, slot_pos = positions[0:1, :], positions[1:2, :]
    rest = text_pos & 15
    row = (text_pos >> 4) * 8 + (rest & 7)
    block_of_image = lax.broadcasted_iota(jnp.int32, (1, 512), 1) // 256
    place = (slot_pos + block_of_image * 4) * 128 + row
    place = jnp.where((rest >> 3) == core, place, -1)

    def logits_of(block):
        low, high = BLOCK_COLUMNS[block]
        for w in range(4):
            slot = block * 4 + w
            products[slot * 128 : (slot + 1) * 128, :] = (
                texts[...] * window_ref[slot : slot + 1, :]
            ).astype(BF16)
        return lax.dot_general(
            products[block * 512 : (block + 1) * 512, :],
            half_ref[low:high, :],
            (((1,), (1,)), ((), ())),
            preferred_element_type=F32,
        )

    def slope_of(block, dots):
        low, high = BLOCK_COLUMNS[block]
        rows = lax.broadcasted_iota(jnp.int32, dots.shape, 0) + block * 512
        positive = rows == place[:, low:high]
        value = jax.nn.sigmoid(temper * dots + offset)
        slope = (temper * jnp.where(positive, value - 1.0, value)).astype(BF16)
        slope_ref[block * 512 : (block + 1) * 512, low:high] = slope
        return slope

    def grads_of(block, slope):
        low, high = BLOCK_COLUMNS[block]
        grads = jnp.dot(slope, half_ref[low:high, :], preferred_element_type=F32)
        part = None
        for w in range(4):
            slot = block * 4 + w
            grad = grads[w * 128 : (w + 1) * 128, :]
            more = grad * window_ref[slot : slot + 1, :]
            part = more if part is None else part + more
            audio_sum[slot : slot + 1, :] = jnp.sum(grad * texts[...], axis=0, keepdims=True)
        return part

    dots = logits_of(0)
    total = None
    for block in range(4):
        slope = slope_of(block, dots)
        if block < 3:
            dots = logits_of(block + 1)
        part = grads_of(block, slope)
        total = part if total is None else total + part
    for c in range(8):
        tiles = total[:, c * 128 : (c + 1) * 128].reshape(16, 8, 128)
        text_ref[c * 2] = tiles[:, 0:4, :]
        text_ref[c * 2 + 1] = tiles[:, 4:8, :]
    first = core == 0
    for level in range(2):
        even = audio_sum[level * 8 : level * 8 + 4, :]
        odd = audio_sum[level * 8 + 4 : level * 8 + 8, :]
        keep_ref[level * 4 : level * 4 + 4, :] = jnp.where(first, even, odd)
        send_ref[level * 4 : level * 4 + 4, :] = jnp.where(first, odd, even)


def image_kernel(core_ref, texts, window_ref, slope_ref, own_ref, other_ref, products):
    core = core_ref[0]
    for slot in range(16):
        products[slot * 128 : (slot + 1) * 128, :] = (
            texts[...] * window_ref[slot : slot + 1, :]
        ).astype(BF16)
    grads = [
        lax.dot_general(
            slope_ref[n * 512 : n * 512 + 1536, n * 256 : (n + 1) * 256],
            products[n * 512 : n * 512 + 1536, :],
            (((0,), (0,)), ((), ())),
            preferred_element_type=F32,
        )
        for n in range(2)
    ]
    first = core == 0
    own_ref[...] = jnp.where(first, grads[0], grads[1])
    other_ref[...] = jnp.where(first, grads[1], grads[0])


def second_kernel(parts_ref, own_ref, came_ref, home_ref, out_ref):
    total = parts_ref[0]
    for n in range(1, 16):
        total = total + parts_ref[n]
    audio = own_ref[0:4, :] + came_ref[0:4, :] + home_ref[...]
    for c in range(8):
        rows = audio[:, c * 128 : (c + 1) * 128]
        out_ref[:, c * 4 : c * 4 + 4, :] = jnp.broadcast_to(rows[None], (16, 4, 128))
    out_ref[:, 32:36, :] = total
    out_ref[:, 36:40, :] = jnp.zeros((16, 4, 128), F32)


def third_kernel(parts_ref, audio_ref, piece_ref):
    total = parts_ref[0]
    for n in range(1, 16):
        total = total + parts_ref[n]
    for c in range(8):
        audio_ref[:, c * 128 : (c + 1) * 128] = total[c * 4 : c * 4 + 4, :]
    piece_ref[...] = jnp.broadcast_to(total[32:36, :][None], (32, 4, 128))


def last_kernel(pieces_ref, out_ref):
    for c in range(8):
        for side in range(2):
            for core in range(2):
                row = core * 8 + side * 4
                out_ref[row : row + 4, c * 128 : (c + 1) * 128] = pieces_ref[(c * 2 + side) * 2 + core]


def call(kernel, outs, specs, scratch=(), flops=0, moved=1 << 20):
    return pl.pallas_call(
        kernel,
        out_shape=[jax.ShapeDtypeStruct(shape, kind) for shape, kind in outs],
        in_specs=specs,
        out_specs=[VMEM] * len(outs),
        scratch_shapes=list(scratch),
        compiler_params=PARAMS,
        cost_estimate=pl.CostEstimate(flops=flops, bytes_accessed=moved, transcendentals=0),
    )


def shards(images, texts, audio, pos_text, pos_audio, logit_scale, logit_bias):
    core = (lax.axis_index("aud") % 2).astype(jnp.int32)
    core_arg = core.reshape(1)
    scalars = jnp.concatenate([logit_scale, logit_bias])

    half_block = lax.dynamic_slice_in_dim(texts, core * 8, 8, 0)
    spread = jnp.broadcast_to(half_block[None], (N_TXT, 8, 1024))
    gathered = lax.all_to_all(spread, BOTH, 0, 0, tiled=True, axis_index_groups=TEXT_GROUPS)
    gathered = gathered.reshape(128, 1024)

    positions = jnp.stack([pos_text, pos_audio])
    other_images = lax.ppermute(images, "aud", OTHER_CORE)
    other_positions = lax.ppermute(positions, "aud", OTHER_CORE)
    far_audio = lax.ppermute(audio, "aud", OTHER_CORE)
    next_own = lax.ppermute(audio, "aud", FROM_NEXT)
    next_far = lax.ppermute(audio, "aud", FROM_NEXT_OTHER)

    half, window = call(
        prepare_kernel,
        [((512, 1024), BF16), ((16, 1024), F32)],
        [SMEM] + [VMEM] * 6,
        moved=3 << 20,
    )(core_arg, images, other_images, audio, far_audio, next_own, next_far)

    slope, text_parts, keep, send = call(
        slope_kernel,
        [((2048, 512), BF16), ((16, 16, 4, 128), F32), ((8, 1024), F32), ((8, 1024), F32)],
        [SMEM, SMEM] + [VMEM] * 5,
        [pltpu.VMEM((2048, 1024), BF16), pltpu.VMEM((16, 1024), F32)],
        flops=3_300_000_000,
        moved=4 << 20,
    )(core_arg, scalars, gathered, half, window, positions, other_positions)

    parts = lax.all_to_all(text_parts, BOTH, 0, 0, tiled=True, axis_index_groups=CHIP_GROUPS)

    came = lax.ppermute(send, "aud", OTHER_CORE)
    home = lax.ppermute(keep[4:8] + came[4:8], "aud", TO_NEXT)

    own_grad, other_grad = call(
        image_kernel,
        [((256, 1024), F32), ((256, 1024), F32)],
        [SMEM] + [VMEM] * 3,
        [pltpu.VMEM((2048, 1024), BF16)],
        flops=1_700_000_000,
        moved=5 << 20,
    )(core_arg, gathered, window, slope)
    grad_images = own_grad + lax.ppermute(other_grad, "aud", OTHER_CORE)

    (second,) = call(second_kernel, [((16, 40, 128), F32)], [VMEM] * 4)(parts, keep, came, home)
    second = lax.all_to_all(second, "txt", 0, 0, tiled=True)
    grad_audio, piece = call(
        third_kernel, [((4, 1024), F32), ((32, 4, 128), F32)], [VMEM]
    )(second)
    pieces = lax.all_to_all(piece, "aud", 0, 0, tiled=True)
    (grad_texts,) = call(last_kernel, [((16, 1024), F32)], [VMEM])(pieces)
    return (grad_images, grad_texts, grad_audio)


def solution(mesh):
    placed = (
        P(("txt", "aud"), None),
        P("txt", None),
        P("aud", None),
        P(("txt", "aud")),
        P(("txt", "aud")),
        P(),
        P(),
    )
    return jax.shard_map(
        shards,
        mesh=mesh,
        in_specs=placed,
        out_specs=(P(("txt", "aud"), None), P("txt", None), P("aud", None)),
        check_vma=False,
    )
```

```python
import jax
import jax.numpy as jnp
from jax import lax
from jax.experimental import pallas as pl
from jax.experimental.pallas import tpu as pltpu
from jax.sharding import PartitionSpec as P

BOTH = ("txt", "aud")
N_TXT, N_AUD = 16, 32
F32, BF16 = jnp.float32, jnp.bfloat16
VMEM = pl.BlockSpec(memory_space=pltpu.VMEM)
SMEM = pl.BlockSpec(memory_space=pltpu.SMEM)


def device(high, z, x, low, core):
    return (high * 8 + z) * N_AUD + (x * 4 + low) * 2 + core


def groups_by(key):
    found = {}
    for high in range(2):
        for z in range(8):
            for x in range(4):
                for low in range(4):
                    for core in range(2):
                        place = (high, z, x, low, core)
                        found.setdefault(key(*place), []).append(device(*place))
    return [found[k] for k in sorted(found)]


TEXT_GROUPS = groups_by(lambda high, z, x, low, core: (x, low if high == 0 else low ^ 2, core))
Y_GROUPS = groups_by(lambda high, z, x, low, core: (z, x, core))
Z_GROUPS = groups_by(lambda high, z, x, low, core: (high, x, low, core))

OTHER_CORE = [(i, i ^ 1) for i in range(N_AUD)]
FROM_NEXT = [(i, (i - 2) % N_AUD) for i in range(N_AUD)]
OTHER_HALF = [(i, i ^ 8) for i in range(N_TXT)]
TO_NEXT = [(i, (i + 2) % N_AUD) for i in range(N_AUD)]


BLOCK_COLUMNS = ((0, 256), (0, 512), (0, 512), (256, 512))


def slope_kernel(
    core_ref, scalar_ref, texts, own_ref, other_a, other_b, own_small, far_small, next_pair,
    slope_out, text_ref, keep_ref, send_ref, window_ref,
    half_ref, slope_ref, products, audio_sum, sems,
):
    core = core_ref[0]
    first = core == 0
    temper, offset = scalar_ref[0], scalar_ref[1]
    for level, (a, b) in enumerate(
        ((own_small[0:4, :], far_small[0:4, :]), (next_pair[0:4, :], next_pair[4:8, :]))
    ):
        window_ref[level * 8 : level * 8 + 4, :] = jnp.where(first, a, b)
        window_ref[level * 8 + 4 : level * 8 + 8, :] = jnp.where(first, b, a)
    half_ref[pl.ds(pl.multiple_of(core * 256, 256), 256), :] = own_ref[...].astype(BF16)
    half_ref[pl.ds(pl.multiple_of((1 - core) * 256, 256), 128), :] = other_a[...].astype(BF16)
    half_ref[pl.ds(pl.multiple_of((1 - core) * 256 + 128, 128), 128), :] = other_b[...].astype(BF16)
    own, far = own_small[4:5, :].astype(jnp.int32), far_small[4:5, :].astype(jnp.int32)
    low, high = jnp.where(first, own, far), jnp.where(first, far, own)
    text_pos = jnp.concatenate([low[:, 0:256], high[:, 0:256]], axis=1)
    slot_pos = jnp.concatenate([low[:, 256:512], high[:, 256:512] + 4], axis=1)
    rest = text_pos & 15
    place = slot_pos * 128 + (text_pos >> 4) * 8 + (rest & 7)
    place = jnp.where((rest >> 3) == core, place, -1)

    def slope_copy(block):
        low, high = BLOCK_COLUMNS[block]
        where = (pl.ds(block * 512, 512), pl.ds(low, high - low))
        return pltpu.make_async_copy(slope_ref.at[where], slope_out.at[where], sems.at[block])

    def logits_of(block):
        low, high = BLOCK_COLUMNS[block]
        for w in range(4):
            slot = block * 4 + w
            products[slot * 128 : (slot + 1) * 128, :] = (
                texts[...] * window_ref[slot : slot + 1, :]
            ).astype(BF16)
        return lax.dot_general(
            products[block * 512 : (block + 1) * 512, :],
            half_ref[low:high, :],
            (((1,), (1,)), ((), ())),
            preferred_element_type=F32,
        )

    def slope_of(block, dots):
        low, high = BLOCK_COLUMNS[block]
        rows = lax.broadcasted_iota(jnp.int32, dots.shape, 0) + block * 512
        positive = rows == place[:, low:high]
        value = jax.nn.sigmoid(temper * dots + offset)
        slope = (temper * jnp.where(positive, value - 1.0, value)).astype(BF16)
        slope_ref[block * 512 : (block + 1) * 512, low:high] = slope
        slope_copy(block).start()
        return slope

    def grads_of(block, slope):
        low, high = BLOCK_COLUMNS[block]
        grads = jnp.dot(slope, half_ref[low:high, :], preferred_element_type=F32)
        part = None
        for w in range(4):
            slot = block * 4 + w
            grad = grads[w * 128 : (w + 1) * 128, :]
            more = grad * window_ref[slot : slot + 1, :]
            part = more if part is None else part + more
            audio_sum[slot : slot + 1, :] = jnp.sum(grad * texts[...], axis=0, keepdims=True)
        return part

    dots = logits_of(0)
    total = None
    for block in range(4):
        slope = slope_of(block, dots)
        if block < 3:
            dots = logits_of(block + 1)
        part = grads_of(block, slope)
        total = part if total is None else total + part
    for c in range(8):
        for high in range(2):
            tiles = total[high * 64 : (high + 1) * 64, c * 128 : (c + 1) * 128].reshape(8, 8, 128)
            text_ref[high * 4 + c // 2, :, (c % 2) * 8 : (c % 2) * 8 + 8, :] = tiles
    for level in range(2):
        even = audio_sum[level * 8 : level * 8 + 4, :]
        odd = audio_sum[level * 8 + 4 : level * 8 + 8, :]
        keep_ref[level * 4 : level * 4 + 4, :] = jnp.where(first, even, odd)
        send_ref[level * 4 : level * 4 + 4, :] = jnp.where(first, odd, even)
    for block in range(4):
        slope_copy(block).wait()


def image_kernel(core_ref, texts, window_ref, slope_ref, own_ref, other_a, other_b, products):
    core = core_ref[0]
    for slot in range(16):
        products[slot * 128 : (slot + 1) * 128, :] = (
            texts[...] * window_ref[slot : slot + 1, :]
        ).astype(BF16)
    grads = [
        lax.dot_general(
            slope_ref[n * 512 : n * 512 + 1536, n * 256 : (n + 1) * 256],
            products[n * 512 : n * 512 + 1536, :],
            (((0,), (0,)), ((), ())),
            preferred_element_type=F32,
        )
        for n in range(2)
    ]
    first = core == 0
    own_ref[...] = jnp.where(first, grads[0], grads[1])
    other_a[...] = jnp.where(first, grads[1][0:128], grads[0][0:128])
    other_b[...] = jnp.where(first, grads[1][128:256], grads[0][128:256])


def second_kernel(parts_ref, own_ref, came_ref, home_ref, out_ref):
    total = parts_ref[0]
    for n in range(1, 8):
        total = total + parts_ref[n]
    out_ref[:, 0:16, :] = total
    audio = own_ref[0:4, :] + came_ref[0:4, :] + home_ref[...]
    for c in range(8):
        rows = audio[:, c * 128 : (c + 1) * 128]
        out_ref[:, 16 + c * 4 : 20 + c * 4, :] = jnp.broadcast_to(rows[None], (8, 4, 128))


def third_kernel(parts_ref, audio_ref, piece_ref):
    total = parts_ref[0]
    for n in range(1, 8):
        total = total + parts_ref[n]
    for c in range(8):
        audio_ref[:, c * 128 : (c + 1) * 128] = total[16 + c * 4 : 20 + c * 4, :]
    piece_ref[...] = jnp.broadcast_to(total[0:16, :][None], (32, 16, 128))


def last_kernel(pieces_ref, mine_ref, fixed_ref, out_ref, audio_ref):
    audio_ref[...] = mine_ref[...] + fixed_ref[...]
    for core in range(2):
        for low in range(4):
            total = pieces_ref[low * 2 + core]
            for x in range(1, 4):
                total = total + pieces_ref[(x * 4 + low) * 2 + core]
            for n in range(2):
                left = (low * 2 + n) * 128
                out_ref[core * 8 : core * 8 + 8, left : left + 128] = total[n * 8 : n * 8 + 8, :]


def call(kernel, outs, specs, scratch=(), flops=0, moved=1 << 20, room=4, out_specs=None):
    return pl.pallas_call(
        kernel,
        out_shape=[o if hasattr(o, "shape") else jax.ShapeDtypeStruct(*o) for o in outs],
        in_specs=specs,
        out_specs=out_specs or [VMEM] * len(outs),
        scratch_shapes=list(scratch),
        compiler_params=pltpu.CompilerParams(vmem_limit_bytes=room << 20),
        cost_estimate=pl.CostEstimate(flops=flops, bytes_accessed=moved, transcendentals=0),
    )


def shards(images, texts, audio, pos_text, pos_audio, logit_scale, logit_bias):
    core = (lax.axis_index("aud") % 2).astype(jnp.int32)
    core_arg = core.reshape(1)
    scalars = jnp.concatenate([logit_scale, logit_bias])

    half_block = lax.dynamic_slice_in_dim(texts, core * 8, 8, 0)
    spread = jnp.broadcast_to(half_block[None], (N_TXT, 8, 1024))
    spread, audio = lax.optimization_barrier((spread, audio))
    gathered = lax.all_to_all(spread, BOTH, 0, 0, tiled=True, axis_index_groups=TEXT_GROUPS)
    gathered = gathered.reshape(128, 1024)

    small = jnp.concatenate(
        [audio, jnp.concatenate([pos_text, pos_audio, jnp.zeros((512,), jnp.int32)]).astype(F32)[None]]
    )
    far_small = lax.ppermute(small, "aud", OTHER_CORE)
    next_pair = lax.ppermute(jnp.concatenate([audio, far_small[0:4]]), "aud", FROM_NEXT)
    other_a = lax.ppermute(images[0:128], "aud", OTHER_CORE)
    other_b = lax.ppermute(images[128:256], "aud", OTHER_CORE)

    slope, text_parts, keep, send, window = call(
        slope_kernel,
        [
            pltpu.HBM((2048, 512), BF16),
            ((8, 8, 16, 128), F32),
            ((8, 1024), F32),
            ((8, 1024), F32),
            ((16, 1024), F32),
        ],
        [SMEM, SMEM] + [VMEM] * 7,
        [
            pltpu.VMEM((512, 1024), BF16),
            pltpu.VMEM((2048, 512), BF16),
            pltpu.VMEM((2048, 1024), BF16),
            pltpu.VMEM((16, 1024), F32),
            pltpu.SemaphoreType.DMA((4,)),
        ],
        flops=3_300_000_000,
        moved=4 << 20,
        room=26,
        out_specs=[pl.BlockSpec(memory_space=pltpu.HBM)] + [VMEM] * 4,
    )(core_arg, scalars, gathered, images, other_a, other_b, small, far_small, next_pair)

    parts = lax.all_to_all(text_parts, BOTH, 0, 0, tiled=True, axis_index_groups=Y_GROUPS)

    came = lax.ppermute(send, "aud", OTHER_CORE)
    leaving = keep[4:8] + came[4:8]
    home = lax.ppermute(leaving, "aud", TO_NEXT)

    (second,) = call(second_kernel, [((8, 48, 128), F32)], [VMEM] * 4)(parts, keep, came, home)
    slope = lax.optimization_barrier((slope, second))[0]
    second = lax.all_to_all(second, BOTH, 0, 0, tiled=True, axis_index_groups=Z_GROUPS)
    own_grad, *other_grads = call(
        image_kernel,
        [((256, 1024), F32), ((128, 1024), F32), ((128, 1024), F32)],
        [SMEM] + [VMEM] * 3,
        [pltpu.VMEM((2048, 1024), BF16)],
        flops=1_700_000_000,
        moved=5 << 20,
        room=24,
    )(core_arg, gathered, window, slope)
    mine, piece = call(
        third_kernel, [((4, 1024), F32), ((32, 16, 128), F32)], [VMEM]
    )(second)
    pieces = lax.all_to_all(piece, "aud", 0, 0, tiled=True)
    fixed = lax.ppermute(mine, "txt", OTHER_HALF)
    came_grads = [lax.ppermute(grad, "aud", OTHER_CORE) for grad in other_grads]
    grad_images = own_grad + jnp.concatenate(came_grads)
    fixed, grad_images = lax.optimization_barrier((fixed, grad_images))
    grad_texts, grad_audio = call(
        last_kernel, [((16, 1024), F32), ((4, 1024), F32)], [VMEM] * 3
    )(pieces, mine, fixed)
    return (grad_images, grad_texts, grad_audio)


def solution(mesh):
    placed = (
        P(("txt", "aud"), None),
        P("txt", None),
        P("aud", None),
        P(("txt", "aud")),
        P(("txt", "aud")),
        P(),
        P(),
    )
    return jax.shard_map(
        shards,
        mesh=mesh,
        in_specs=placed,
        out_specs=(P(("txt", "aud"), None), P("txt", None), P("aud", None)),
        check_vma=False,
    )
```

```python
import jax
import jax.numpy as jnp
from jax import lax
from jax.experimental import pallas as pl
from jax.experimental.pallas import tpu as pltpu
from jax.sharding import PartitionSpec as P

BOTH = ("txt", "aud")
N_TXT, N_AUD = 16, 32
SPLIT = 128
F32, BF16 = jnp.float32, jnp.bfloat16
VMEM = pl.BlockSpec(memory_space=pltpu.VMEM)
SMEM = pl.BlockSpec(memory_space=pltpu.SMEM)


def device(high, z, x, low, core):
    return (high * 8 + z) * N_AUD + (x * 4 + low) * 2 + core


def groups_by(key):
    found = {}
    for high in range(2):
        for z in range(8):
            for x in range(4):
                for low in range(4):
                    for core in range(2):
                        place = (high, z, x, low, core)
                        found.setdefault(key(*place), []).append(device(*place))
    return [found[k] for k in sorted(found)]


TEXT_GROUPS = groups_by(lambda high, z, x, low, core: (x, low if high == 0 else low ^ 2, core))
Y_GROUPS = groups_by(lambda high, z, x, low, core: (z, x, core))
Z_GROUPS = groups_by(lambda high, z, x, low, core: (high, x, low, core))

OTHER_CORE = [(i, i ^ 1) for i in range(N_AUD)]
FROM_NEXT = [(i, (i - 2) % N_AUD) for i in range(N_AUD)]
OTHER_HALF = [(i, i ^ 8) for i in range(N_TXT)]
TO_NEXT = [(i, (i + 2) % N_AUD) for i in range(N_AUD)]
TO_NEXT_OTHER = [(i, ((i + 2) % N_AUD) ^ 1) for i in range(N_AUD)]


BLOCK_COLUMNS = ((0, 256), (0, 512), (0, 512), (256, 512))


def pack_kernel(images_ref, audio_ref, text_ref, slot_ref, first_ref, rest_ref):
    first_ref[0:SPLIT, :] = images_ref[0:SPLIT, :]
    rest_ref[...] = images_ref[SPLIT:256, :]
    first_ref[SPLIT : SPLIT + 8, :] = jnp.zeros((8, 1024), F32)
    first_ref[SPLIT : SPLIT + 4, :] = audio_ref[...]
    first_ref[SPLIT + 4 : SPLIT + 5, 0:256] = text_ref[...].astype(F32)
    first_ref[SPLIT + 4 : SPLIT + 5, 256:512] = slot_ref[...].astype(F32)


def pair_kernel(own_ref, far_ref, pair_ref):
    pair_ref[0:4, :] = own_ref[0:4, :]
    pair_ref[4:8, :] = far_ref[0:4, :]


def slope_kernel(
    core_ref, scale_ref, bias_ref, texts, own_a, own_b, other_a, other_b, next_pair,
    slope_out, text_ref, keep_self, keep_next, send_self, send_next, window_ref,
    half_ref, slope_ref, products, audio_sum, total, sems,
):
    core = core_ref[0]
    first = core == 0
    temper, offset = scale_ref[0], bias_ref[0]
    for level, (a, b) in enumerate(
        ((own_a[SPLIT : SPLIT + 4, :], other_a[SPLIT : SPLIT + 4, :]), (next_pair[0:4, :], next_pair[4:8, :]))
    ):
        window_ref[level * 8 : level * 8 + 4, :] = jnp.where(first, a, b)
        window_ref[level * 8 + 4 : level * 8 + 8, :] = jnp.where(first, b, a)
    for which, a, b in ((core, own_a, own_b), (1 - core, other_a, other_b)):
        top = pl.multiple_of(which * 256, 256)
        middle = pl.multiple_of(which * 256 + SPLIT, 32)
        half_ref[pl.ds(top, SPLIT), :] = a[0:SPLIT, :].astype(BF16)
        half_ref[pl.ds(middle, 256 - SPLIT), :] = b[...].astype(BF16)
    own = own_a[SPLIT + 4 : SPLIT + 5, :].astype(jnp.int32)
    far = other_a[SPLIT + 4 : SPLIT + 5, :].astype(jnp.int32)
    low, high = jnp.where(first, own, far), jnp.where(first, far, own)
    text_pos = jnp.concatenate([low[:, 0:256], high[:, 0:256]], axis=1)
    slot_pos = jnp.concatenate([low[:, 256:512], high[:, 256:512] + 4], axis=1)
    rest = text_pos & 15
    place = slot_pos * 128 + (text_pos >> 4) * 8 + (rest & 7)
    place = jnp.where((rest >> 3) == core, place, -1)

    def slope_copy(block):
        low, high = BLOCK_COLUMNS[block]
        where = (pl.ds(block * 512, 512), pl.ds(low, high - low))
        return pltpu.make_async_copy(slope_ref.at[where], slope_out.at[where], sems.at[block])

    def logits_of(block):
        low, high = BLOCK_COLUMNS[block]
        for w in range(4):
            slot = block * 4 + w
            row = window_ref[slot : slot + 1, :]
            for r in range(0, 128, 32):
                products[slot * 128 + r : slot * 128 + r + 32, :] = (
                    texts[r : r + 32, :] * row
                ).astype(BF16)
        return lax.dot_general(
            products[block * 512 : (block + 1) * 512, :],
            half_ref[low:high, :],
            (((1,), (1,)), ((), ())),
            preferred_element_type=F32,
        )

    def slope_of(block, dots):
        low, high = BLOCK_COLUMNS[block]
        place_here = place[:, low:high] - block * 512
        for r in range(0, 512, 32):
            rows = lax.broadcasted_iota(jnp.int32, (32, high - low), 0) + r
            value = jax.nn.sigmoid(temper * dots[r : r + 32, :] + offset)
            value = temper * jnp.where(rows == place_here, value - 1.0, value)
            slope_ref[block * 512 + r : block * 512 + r + 32, low:high] = value.astype(BF16)
        slope_copy(block).start()

    def grads_of(block):
        low, high = BLOCK_COLUMNS[block]
        slope = slope_ref[block * 512 : (block + 1) * 512, low:high]
        for n in range(0, 1024, 256):
            grads = jnp.dot(slope, half_ref[low:high, n : n + 256], preferred_element_type=F32)
            for c in range(n, n + 256, 128):
                part = None if block == 0 else total[:, c : c + 128]
                text = texts[:, c : c + 128]
                for w in range(4):
                    slot = block * 4 + w
                    grad = grads[w * 128 : (w + 1) * 128, c - n : c - n + 128]
                    more = grad * window_ref[slot : slot + 1, c : c + 128]
                    part = more if part is None else part + more
                    audio_sum[slot : slot + 1, c : c + 128] = jnp.sum(grad * text, axis=0, keepdims=True)
                if block < 3:
                    total[:, c : c + 128] = part
                    continue
                for high_half in range(2):
                    top = c // 128 % 2 * 8
                    text_ref[high_half * 4 + c // 256, :, top : top + 8, :] = part[
                        high_half * 64 : (high_half + 1) * 64, :
                    ].reshape(8, 8, 128)

    dots = logits_of(0)
    for block in range(4):
        slope_of(block, dots)
        if block < 3:
            dots = logits_of(block + 1)
        grads_of(block)
    for level, (keep_ref, send_ref) in enumerate(((keep_self, send_self), (keep_next, send_next))):
        even = audio_sum[level * 8 : level * 8 + 4, :]
        odd = audio_sum[level * 8 + 4 : level * 8 + 8, :]
        keep_ref[...] = jnp.where(first, even, odd)
        send_ref[...] = jnp.where(first, odd, even)
    for block in range(4):
        slope_copy(block).wait()


def image_kernel(
    core_ref, texts, window_ref, slope_hbm, own_ref, other_a, other_b, products, slope_ref, sems
):
    core = core_ref[0]

    def slope_copy(n):
        where = (pl.ds(n * 512, 1536), pl.ds(n * 256, 256))
        return pltpu.make_async_copy(slope_hbm.at[where], slope_ref.at[where], sems.at[n])

    slope_copy(0).start()
    slope_copy(1).start()
    for slot in range(16):
        products[slot * 128 : (slot + 1) * 128, :] = (
            texts[...] * window_ref[slot : slot + 1, :]
        ).astype(BF16)
    slope_copy(0).wait()
    slope_copy(1).wait()
    grads = [
        lax.dot_general(
            slope_ref[n * 512 : n * 512 + 1536, n * 256 : (n + 1) * 256],
            products[n * 512 : n * 512 + 1536, :],
            (((0,), (0,)), ((), ())),
            preferred_element_type=F32,
        )
        for n in range(2)
    ]
    first = core == 0
    own_ref[...] = jnp.where(first, grads[0], grads[1])
    other_a[...] = jnp.where(first, grads[1][0:128], grads[0][0:128])
    other_b[...] = jnp.where(first, grads[1][128:256], grads[0][128:256])


def second_kernel(parts_ref, own_ref, next_ref, far_ref, came_ref, out_ref):
    total = parts_ref[0]
    for n in range(1, 8):
        total = total + parts_ref[n]
    out_ref[:, 0:16, :] = total
    audio = (own_ref[...] + came_ref[...]) + (next_ref[...] + far_ref[...])
    for c in range(8):
        rows = audio[:, c * 128 : (c + 1) * 128]
        out_ref[:, 16 + c * 4 : 20 + c * 4, :] = jnp.broadcast_to(rows[None], (8, 4, 128))


def third_kernel(parts_ref, audio_ref, piece_ref):
    total = parts_ref[0]
    for n in range(1, 8):
        total = total + parts_ref[n]
    for c in range(8):
        audio_ref[:, c * 128 : (c + 1) * 128] = total[16 + c * 4 : 20 + c * 4, :]
    piece_ref[...] = jnp.broadcast_to(total[0:16, :][None], (32, 16, 128))


def last_kernel(pieces_ref, mine_ref, fixed_ref, out_ref, audio_ref):
    audio_ref[...] = mine_ref[...] + fixed_ref[...]
    for core in range(2):
        for low in range(4):
            total = pieces_ref[low * 2 + core]
            for x in range(1, 4):
                total = total + pieces_ref[(x * 4 + low) * 2 + core]
            for n in range(2):
                left = (low * 2 + n) * 128
                out_ref[core * 8 : core * 8 + 8, left : left + 128] = total[n * 8 : n * 8 + 8, :]


def call(kernel, outs, specs, scratch=(), flops=0, moved=1 << 20, room=4, out_specs=None):
    return pl.pallas_call(
        kernel,
        out_shape=[o if hasattr(o, "shape") else jax.ShapeDtypeStruct(*o) for o in outs],
        in_specs=specs,
        out_specs=out_specs or [VMEM] * len(outs),
        scratch_shapes=list(scratch),
        compiler_params=pltpu.CompilerParams(vmem_limit_bytes=room << 20),
        cost_estimate=pl.CostEstimate(flops=flops, bytes_accessed=moved, transcendentals=0),
    )


def shards(images, texts, audio, pos_text, pos_audio, logit_scale, logit_bias):
    core = (lax.axis_index("aud") % 2).astype(jnp.int32)
    core_arg = core.reshape(1)

    half_block = lax.dynamic_slice_in_dim(texts, core * 8, 8, 0)
    spread = jnp.broadcast_to(half_block[None], (N_TXT, 8, 1024))
    spread, audio = lax.optimization_barrier((spread, audio))
    gathered = lax.all_to_all(spread, BOTH, 0, 0, tiled=True, axis_index_groups=TEXT_GROUPS)
    gathered = gathered.reshape(128, 1024)

    own_a, own_b = call(
        pack_kernel, [((SPLIT + 8, 1024), F32), ((256 - SPLIT, 1024), F32)], [VMEM] * 4
    )(*(pltpu.with_memory_space_constraint(v, pltpu.HBM) for v in (images, audio, pos_text.reshape(1, 256), pos_audio.reshape(1, 256))))
    other_a = lax.ppermute(own_a, "aud", OTHER_CORE)
    other_b = lax.ppermute(own_b, "aud", OTHER_CORE)
    small = pl.BlockSpec((8, 1024), lambda i: (SPLIT // 8, 0))
    pair = pl.pallas_call(
        pair_kernel,
        out_shape=jax.ShapeDtypeStruct((8, 1024), F32),
        grid=(1,),
        in_specs=[small, small],
        out_specs=pl.BlockSpec((8, 1024), lambda i: (0, 0)),
        compiler_params=pltpu.CompilerParams(vmem_limit_bytes=1 << 20),
    )(own_a, other_a)
    next_pair = lax.ppermute(pair, "aud", FROM_NEXT)

    slope, text_parts, keep_self, keep_next, send_self, send_next, window = call(
        slope_kernel,
        [
            pltpu.HBM((2048, 512), BF16),
            ((8, 8, 16, 128), F32),
            ((4, 1024), F32),
            ((4, 1024), F32),
            ((4, 1024), F32),
            ((4, 1024), F32),
            ((16, 1024), F32),
        ],
        [SMEM] * 3 + [VMEM] * 6,
        [
            pltpu.VMEM((512, 1024), BF16),
            pltpu.VMEM((2048, 512), BF16),
            pltpu.VMEM((2048, 1024), BF16),
            pltpu.VMEM((16, 1024), F32),
            pltpu.VMEM((128, 1024), F32),
            pltpu.SemaphoreType.DMA((4,)),
        ],
        flops=3_300_000_000,
        moved=4 << 20,
        room=26,
        out_specs=[pl.BlockSpec(memory_space=pltpu.HBM)] + [VMEM] * 6,
    )(core_arg, logit_scale, logit_bias, gathered, own_a, own_b, other_a, other_b, next_pair)

    parts = lax.all_to_all(text_parts, BOTH, 0, 0, tiled=True, axis_index_groups=Y_GROUPS)

    home = [
        lax.ppermute(keep_next, "aud", TO_NEXT),
        lax.ppermute(send_next, "aud", TO_NEXT_OTHER),
        lax.ppermute(send_self, "aud", OTHER_CORE),
    ]
    window = lax.optimization_barrier((window, home[2]))[0]

    own_grad, *other_grads = call(
        image_kernel,
        [((256, 1024), F32), ((128, 1024), F32), ((128, 1024), F32)],
        [SMEM, VMEM, VMEM, pl.BlockSpec(memory_space=pltpu.HBM)],
        [
            pltpu.VMEM((2048, 1024), BF16),
            pltpu.VMEM((2048, 512), BF16),
            pltpu.SemaphoreType.DMA((2,)),
        ],
        flops=1_700_000_000,
        moved=5 << 20,
        room=24,
    )(core_arg, gathered, window, pltpu.with_memory_space_constraint(slope, pltpu.HBM))
    keep_self, *other_grads = lax.optimization_barrier((keep_self, *other_grads))
    (second,) = call(second_kernel, [((8, 48, 128), F32)], [VMEM] * 5)(parts, keep_self, *home)
    other_grads = lax.optimization_barrier((*other_grads, second))[:2]
    second = lax.all_to_all(second, BOTH, 0, 0, tiled=True, axis_index_groups=Z_GROUPS)
    mine, piece = call(
        third_kernel, [((4, 1024), F32), ((32, 16, 128), F32)], [VMEM]
    )(second)
    pieces = lax.all_to_all(piece, "aud", 0, 0, tiled=True)
    fixed = lax.ppermute(mine, "txt", OTHER_HALF)
    came_grads = [lax.ppermute(grad, "aud", OTHER_CORE) for grad in other_grads]
    grad_images = own_grad + jnp.concatenate(came_grads)
    fixed, grad_images = lax.optimization_barrier((fixed, grad_images))
    grad_texts, grad_audio = call(
        last_kernel, [((16, 1024), F32), ((4, 1024), F32)], [VMEM] * 3
    )(pieces, mine, fixed)
    return (grad_images, grad_texts, grad_audio)


def solution(mesh):
    placed = (
        P(("txt", "aud"), None),
        P("txt", None),
        P("aud", None),
        P(("txt", "aud")),
        P(("txt", "aud")),
        P(),
        P(),
    )
    return jax.shard_map(
        shards,
        mesh=mesh,
        in_specs=placed,
        out_specs=(P(("txt", "aud"), None), P("txt", None), P("aud", None)),
        check_vma=False,
    )
```

```python
import jax
import jax.numpy as jnp
from jax import lax
from jax.experimental import pallas as pl
from jax.experimental.pallas import tpu as pltpu
from jax.sharding import PartitionSpec as P

BOTH = ("txt", "aud")
N_TXT, N_AUD = 16, 32
SPLIT = 128
F32, BF16 = jnp.float32, jnp.bfloat16
VMEM = pl.BlockSpec(memory_space=pltpu.VMEM)
SMEM = pl.BlockSpec(memory_space=pltpu.SMEM)


def device(high, z, x, low, core):
    return (high * 8 + z) * N_AUD + (x * 4 + low) * 2 + core


def groups_by(key):
    found = {}
    for high in range(2):
        for z in range(8):
            for x in range(4):
                for low in range(4):
                    for core in range(2):
                        place = (high, z, x, low, core)
                        found.setdefault(key(*place), []).append(device(*place))
    return [found[k] for k in sorted(found)]


TEXT_GROUPS = groups_by(lambda high, z, x, low, core: (x, low if high == 0 else 3 - low, core))
Y_GROUPS = groups_by(lambda high, z, x, low, core: (z, x, core))
Z_GROUPS = groups_by(lambda high, z, x, low, core: (high, x, low, core))

OTHER_CORE = [(i, i ^ 1) for i in range(N_AUD)]
FROM_NEXT = [(i, (i - 2) % N_AUD) for i in range(N_AUD)]
OTHER_HALF = [(i, i ^ 8) for i in range(N_TXT)]
TO_NEXT = [(i, (i + 2) % N_AUD) for i in range(N_AUD)]
TO_NEXT_OTHER = [(i, ((i + 2) % N_AUD) ^ 1) for i in range(N_AUD)]


BLOCK_COLUMNS = ((0, 256), (0, 512), (0, 512), (256, 512))


def pack_kernel(images_ref, audio_ref, text_ref, slot_ref, first_ref, rest_ref):
    first_ref[0:SPLIT, :] = images_ref[0:SPLIT, :]
    rest_ref[...] = images_ref[SPLIT:256, :]
    first_ref[SPLIT : SPLIT + 8, :] = jnp.zeros((8, 1024), F32)
    first_ref[SPLIT : SPLIT + 4, :] = audio_ref[...]
    first_ref[SPLIT + 4 : SPLIT + 5, 0:256] = text_ref[...].astype(F32)
    first_ref[SPLIT + 4 : SPLIT + 5, 256:512] = slot_ref[...].astype(F32)


def pair_kernel(own_ref, far_ref, pair_ref):
    pair_ref[0:4, :] = own_ref[0:4, :]
    pair_ref[4:8, :] = far_ref[0:4, :]


def slope_kernel(
    core_ref, scale_ref, bias_ref, texts, own_a, own_b, other_a, other_b, next_pair,
    slope_out, text_ref, keep_self, keep_next, send_self, send_next, window_ref,
    half_ref, slope_ref, products, audio_sum, total, sems,
):
    core = core_ref[0]
    first = core == 0
    temper, offset = scale_ref[0], bias_ref[0]
    for level, (a, b) in enumerate(
        ((own_a[SPLIT : SPLIT + 4, :], other_a[SPLIT : SPLIT + 4, :]), (next_pair[0:4, :], next_pair[4:8, :]))
    ):
        window_ref[level * 8 : level * 8 + 4, :] = jnp.where(first, a, b)
        window_ref[level * 8 + 4 : level * 8 + 8, :] = jnp.where(first, b, a)
    for which, a, b in ((core, own_a, own_b), (1 - core, other_a, other_b)):
        top = pl.multiple_of(which * 256, 256)
        middle = pl.multiple_of(which * 256 + SPLIT, 32)
        half_ref[pl.ds(top, SPLIT), :] = a[0:SPLIT, :].astype(BF16)
        half_ref[pl.ds(middle, 256 - SPLIT), :] = b[...].astype(BF16)
    own = own_a[SPLIT + 4 : SPLIT + 5, :].astype(jnp.int32)
    far = other_a[SPLIT + 4 : SPLIT + 5, :].astype(jnp.int32)
    low, high = jnp.where(first, own, far), jnp.where(first, far, own)
    text_pos = jnp.concatenate([low[:, 0:256], high[:, 0:256]], axis=1)
    slot_pos = jnp.concatenate([low[:, 256:512], high[:, 256:512] + 4], axis=1)
    rest = text_pos & 15
    place = slot_pos * 128 + (text_pos >> 4) * 8 + (rest & 7)
    place = jnp.where((rest >> 3) == core, place, -1)

    def slope_copy(block):
        low, high = BLOCK_COLUMNS[block]
        where = (pl.ds(block * 512, 512), pl.ds(low, high - low))
        return pltpu.make_async_copy(slope_ref.at[where], slope_out.at[where], sems.at[block])

    def logits_of(block):
        low, high = BLOCK_COLUMNS[block]
        for w in range(4):
            slot = block * 4 + w
            row = window_ref[slot : slot + 1, :]
            for r in range(0, 128, 32):
                products[slot * 128 + r : slot * 128 + r + 32, :] = (
                    texts[r : r + 32, :] * row
                ).astype(BF16)
        return lax.dot_general(
            products[block * 512 : (block + 1) * 512, :],
            half_ref[low:high, :],
            (((1,), (1,)), ((), ())),
            preferred_element_type=F32,
        )

    def slope_of(block, dots):
        low, high = BLOCK_COLUMNS[block]
        place_here = place[:, low:high] - block * 512
        for r in range(0, 512, 32):
            rows = lax.broadcasted_iota(jnp.int32, (32, high - low), 0) + r
            value = jax.nn.sigmoid(temper * dots[r : r + 32, :] + offset)
            value = temper * jnp.where(rows == place_here, value - 1.0, value)
            slope_ref[block * 512 + r : block * 512 + r + 32, low:high] = value.astype(BF16)
        slope_copy(block).start()

    def grads_of(block):
        low, high = BLOCK_COLUMNS[block]
        slope = slope_ref[block * 512 : (block + 1) * 512, low:high]
        for n in range(0, 1024, 256):
            grads = jnp.dot(slope, half_ref[low:high, n : n + 256], preferred_element_type=F32)
            for c in range(n, n + 256, 128):
                part = None if block == 0 else total[:, c : c + 128]
                text = texts[:, c : c + 128]
                for w in range(4):
                    slot = block * 4 + w
                    grad = grads[w * 128 : (w + 1) * 128, c - n : c - n + 128]
                    more = grad * window_ref[slot : slot + 1, c : c + 128]
                    part = more if part is None else part + more
                    audio_sum[slot : slot + 1, c : c + 128] = jnp.sum(grad * text, axis=0, keepdims=True)
                if block < 3:
                    total[:, c : c + 128] = part
                    continue
                for high_half in range(2):
                    top = c // 128 % 2 * 8
                    text_ref[high_half * 4 + c // 256, :, top : top + 8, :] = part[
                        high_half * 64 : (high_half + 1) * 64, :
                    ].reshape(8, 8, 128)

    dots = logits_of(0)
    for block in range(4):
        slope_of(block, dots)
        if block < 3:
            dots = logits_of(block + 1)
        grads_of(block)
    for level, (keep_ref, send_ref) in enumerate(((keep_self, send_self), (keep_next, send_next))):
        even = audio_sum[level * 8 : level * 8 + 4, :]
        odd = audio_sum[level * 8 + 4 : level * 8 + 8, :]
        keep_ref[...] = jnp.where(first, even, odd)
        send_ref[...] = jnp.where(first, odd, even)
    for block in range(4):
        slope_copy(block).wait()


def image_kernel(
    core_ref, texts, window_ref, slope_hbm, own_ref, other_a, other_b, products, slope_ref, sems
):
    core = core_ref[0]

    def slope_copy(n):
        where = (pl.ds(n * 512, 1536), pl.ds(n * 256, 256))
        return pltpu.make_async_copy(slope_hbm.at[where], slope_ref.at[where], sems.at[n])

    slope_copy(0).start()
    slope_copy(1).start()
    for slot in range(16):
        products[slot * 128 : (slot + 1) * 128, :] = (
            texts[...] * window_ref[slot : slot + 1, :]
        ).astype(BF16)
    slope_copy(0).wait()
    slope_copy(1).wait()
    grads = [
        lax.dot_general(
            slope_ref[n * 512 : n * 512 + 1536, n * 256 : (n + 1) * 256],
            products[n * 512 : n * 512 + 1536, :],
            (((0,), (0,)), ((), ())),
            preferred_element_type=F32,
        )
        for n in range(2)
    ]
    first = core == 0
    own_ref[...] = jnp.where(first, grads[0], grads[1])
    other_a[...] = jnp.where(first, grads[1][0:128], grads[0][0:128])
    other_b[...] = jnp.where(first, grads[1][128:256], grads[0][128:256])


def second_kernel(parts_ref, own_ref, next_ref, far_ref, came_ref, out_ref):
    total = parts_ref[0]
    for n in range(1, 8):
        total = total + parts_ref[n]
    out_ref[:, 0:16, :] = total
    audio = (own_ref[...] + came_ref[...]) + (next_ref[...] + far_ref[...])
    for c in range(8):
        rows = audio[:, c * 128 : (c + 1) * 128]
        out_ref[:, 16 + c * 4 : 20 + c * 4, :] = jnp.broadcast_to(rows[None], (8, 4, 128))


def third_kernel(parts_ref, audio_ref, piece_ref):
    total = parts_ref[0]
    for n in range(1, 8):
        total = total + parts_ref[n]
    for c in range(8):
        audio_ref[:, c * 128 : (c + 1) * 128] = total[16 + c * 4 : 20 + c * 4, :]
    piece_ref[...] = jnp.broadcast_to(total[0:16, :][None], (32, 16, 128))


def last_kernel(pieces_ref, mine_ref, fixed_ref, out_ref, audio_ref):
    audio_ref[...] = mine_ref[...] + fixed_ref[...]
    for core in range(2):
        for low in range(4):
            total = pieces_ref[low * 2 + core]
            for x in range(1, 4):
                total = total + pieces_ref[(x * 4 + low) * 2 + core]
            for n in range(2):
                left = (low * 2 + n) * 128
                out_ref[core * 8 : core * 8 + 8, left : left + 128] = total[n * 8 : n * 8 + 8, :]


def call(kernel, outs, specs, scratch=(), flops=0, moved=1 << 20, room=4, out_specs=None):
    return pl.pallas_call(
        kernel,
        out_shape=[o if hasattr(o, "shape") else jax.ShapeDtypeStruct(*o) for o in outs],
        in_specs=specs,
        out_specs=out_specs or [VMEM] * len(outs),
        scratch_shapes=list(scratch),
        compiler_params=pltpu.CompilerParams(vmem_limit_bytes=room << 20),
        cost_estimate=pl.CostEstimate(flops=flops, bytes_accessed=moved, transcendentals=0),
    )


def shards(images, texts, audio, pos_text, pos_audio, logit_scale, logit_bias):
    core = (lax.axis_index("aud") % 2).astype(jnp.int32)
    core_arg = core.reshape(1)

    half_block = lax.dynamic_slice_in_dim(texts, core * 8, 8, 0)
    spread = jnp.broadcast_to(half_block[None], (N_TXT, 8, 1024))
    spread, audio = lax.optimization_barrier((spread, audio))
    gathered = lax.all_to_all(spread, BOTH, 0, 0, tiled=True, axis_index_groups=TEXT_GROUPS)
    gathered = gathered.reshape(128, 1024)

    own_a, own_b = call(
        pack_kernel, [((SPLIT + 8, 1024), F32), ((256 - SPLIT, 1024), F32)], [VMEM] * 4
    )(*(pltpu.with_memory_space_constraint(v, pltpu.HBM) for v in (images, audio, pos_text.reshape(1, 256), pos_audio.reshape(1, 256))))
    other_a = lax.ppermute(own_a, "aud", OTHER_CORE)
    other_b = lax.ppermute(own_b, "aud", OTHER_CORE)
    small = pl.BlockSpec((8, 1024), lambda i: (SPLIT // 8, 0))
    pair = pl.pallas_call(
        pair_kernel,
        out_shape=jax.ShapeDtypeStruct((8, 1024), F32),
        grid=(1,),
        in_specs=[small, small],
        out_specs=pl.BlockSpec((8, 1024), lambda i: (0, 0)),
        compiler_params=pltpu.CompilerParams(vmem_limit_bytes=1 << 20),
    )(own_a, other_a)
    next_pair = lax.ppermute(pair, "aud", FROM_NEXT)

    slope, text_parts, keep_self, keep_next, send_self, send_next, window = call(
        slope_kernel,
        [
            pltpu.HBM((2048, 512), BF16),
            ((8, 8, 16, 128), F32),
            ((4, 1024), F32),
            ((4, 1024), F32),
            ((4, 1024), F32),
            ((4, 1024), F32),
            ((16, 1024), F32),
        ],
        [SMEM] * 3 + [VMEM] * 6,
        [
            pltpu.VMEM((512, 1024), BF16),
            pltpu.VMEM((2048, 512), BF16),
            pltpu.VMEM((2048, 1024), BF16),
            pltpu.VMEM((16, 1024), F32),
            pltpu.VMEM((128, 1024), F32),
            pltpu.SemaphoreType.DMA((4,)),
        ],
        flops=3_300_000_000,
        moved=4 << 20,
        room=26,
        out_specs=[pl.BlockSpec(memory_space=pltpu.HBM)] + [VMEM] * 6,
    )(core_arg, logit_scale, logit_bias, gathered, own_a, own_b, other_a, other_b, next_pair)

    parts = lax.all_to_all(text_parts, BOTH, 0, 0, tiled=True, axis_index_groups=Y_GROUPS)

    home = [
        lax.ppermute(keep_next, "aud", TO_NEXT),
        lax.ppermute(send_next, "aud", TO_NEXT_OTHER),
        lax.ppermute(send_self, "aud", OTHER_CORE),
    ]
    window = lax.optimization_barrier((window, home[2]))[0]

    own_grad, *other_grads = call(
        image_kernel,
        [((256, 1024), F32), ((128, 1024), F32), ((128, 1024), F32)],
        [SMEM, VMEM, VMEM, pl.BlockSpec(memory_space=pltpu.HBM)],
        [
            pltpu.VMEM((2048, 1024), BF16),
            pltpu.VMEM((2048, 512), BF16),
            pltpu.SemaphoreType.DMA((2,)),
        ],
        flops=1_700_000_000,
        moved=5 << 20,
        room=24,
    )(core_arg, gathered, window, pltpu.with_memory_space_constraint(slope, pltpu.HBM))
    keep_self, *other_grads = lax.optimization_barrier((keep_self, *other_grads))
    (second,) = call(second_kernel, [((8, 48, 128), F32)], [VMEM] * 5)(parts, keep_self, *home)
    other_grads = lax.optimization_barrier((*other_grads, second))[:2]
    second = lax.all_to_all(second, BOTH, 0, 0, tiled=True, axis_index_groups=Z_GROUPS)
    mine, piece = call(
        third_kernel, [((4, 1024), F32), ((32, 16, 128), F32)], [VMEM]
    )(second)
    pieces = lax.all_to_all(piece, "aud", 0, 0, tiled=True)
    fixed = lax.ppermute(mine, "txt", OTHER_HALF)
    came_grads = [lax.ppermute(grad, "aud", OTHER_CORE) for grad in other_grads]
    grad_images = own_grad + jnp.concatenate(came_grads)
    fixed, grad_images = lax.optimization_barrier((fixed, grad_images))
    grad_texts, grad_audio = call(
        last_kernel, [((16, 1024), F32), ((4, 1024), F32)], [VMEM] * 3
    )(pieces, mine, fixed)
    return (grad_images, grad_texts, grad_audio)


def solution(mesh):
    placed = (
        P(("txt", "aud"), None),
        P("txt", None),
        P("aud", None),
        P(("txt", "aud")),
        P(("txt", "aud")),
        P(),
        P(),
    )
    return jax.shard_map(
        shards,
        mesh=mesh,
        in_specs=placed,
        out_specs=(P(("txt", "aud"), None), P("txt", None), P("aud", None)),
        check_vma=False,
    )
```

```python
import jax
import jax.numpy as jnp
from jax import lax
from jax.experimental import pallas as pl
from jax.experimental.pallas import tpu as pltpu
from jax.sharding import PartitionSpec as P

BOTH = ("txt", "aud")
N_TXT, N_AUD = 16, 32
SPLIT = 128
F32, BF16 = jnp.float32, jnp.bfloat16
VMEM = pl.BlockSpec(memory_space=pltpu.VMEM)
SMEM = pl.BlockSpec(memory_space=pltpu.SMEM)


def device(high, z, x, low, core):
    return (high * 8 + z) * N_AUD + (x * 4 + low) * 2 + core


def groups_by(key):
    found = {}
    for high in range(2):
        for z in range(8):
            for x in range(4):
                for low in range(4):
                    for core in range(2):
                        place = (high, z, x, low, core)
                        found.setdefault(key(*place), []).append(device(*place))
    return [found[k] for k in sorted(found)]


TEXT_GROUPS = [
    [group[p % 2 * 8 + p // 2] for p in range(N_TXT)]
    for group in groups_by(lambda high, z, x, low, core: (x, low if high == 0 else 3 - low, core))
]
Y_GROUPS = groups_by(lambda high, z, x, low, core: (z, x, core))
Z_GROUPS = groups_by(lambda high, z, x, low, core: (high, x, low, core))

OTHER_CORE = [(i, i ^ 1) for i in range(N_AUD)]
FROM_NEXT = [(i, (i - 2) % N_AUD) for i in range(N_AUD)]
OTHER_HALF = [(i, i ^ 8) for i in range(N_TXT)]
TO_NEXT = [(i, (i + 2) % N_AUD) for i in range(N_AUD)]
TO_NEXT_OTHER = [(i, ((i + 2) % N_AUD) ^ 1) for i in range(N_AUD)]


BLOCK_COLUMNS = ((0, 256), (0, 512), (0, 512), (256, 512))


def pack_kernel(images_ref, audio_ref, text_ref, slot_ref, first_ref, rest_ref):
    first_ref[0:SPLIT, :] = images_ref[0:SPLIT, :]
    rest_ref[...] = images_ref[SPLIT:256, :]
    first_ref[SPLIT : SPLIT + 8, :] = jnp.zeros((8, 1024), F32)
    first_ref[SPLIT : SPLIT + 4, :] = audio_ref[...]
    first_ref[SPLIT + 4 : SPLIT + 5, 0:256] = text_ref[...].astype(F32)
    first_ref[SPLIT + 4 : SPLIT + 5, 256:512] = slot_ref[...].astype(F32)


def pair_kernel(own_ref, far_ref, pair_ref):
    pair_ref[0:4, :] = own_ref[0:4, :]
    pair_ref[4:8, :] = far_ref[0:4, :]


def slope_kernel(
    core_ref, scale_ref, bias_ref, texts, own_a, own_b, other_a, other_b, next_pair,
    slope_out, text_ref, keep_self, keep_next, send_self, send_next, window_ref,
    half_ref, slope_ref, products, audio_sum, total, sems,
):
    core = core_ref[0]
    first = core == 0
    temper, offset = scale_ref[0], bias_ref[0]
    for level, (a, b) in enumerate(
        ((own_a[SPLIT : SPLIT + 4, :], other_a[SPLIT : SPLIT + 4, :]), (next_pair[0:4, :], next_pair[4:8, :]))
    ):
        window_ref[level * 8 : level * 8 + 4, :] = jnp.where(first, a, b)
        window_ref[level * 8 + 4 : level * 8 + 8, :] = jnp.where(first, b, a)
    for which, a, b in ((core, own_a, own_b), (1 - core, other_a, other_b)):
        top = pl.multiple_of(which * 256, 256)
        middle = pl.multiple_of(which * 256 + SPLIT, 32)
        half_ref[pl.ds(top, SPLIT), :] = a[0:SPLIT, :].astype(BF16)
        half_ref[pl.ds(middle, 256 - SPLIT), :] = b[...].astype(BF16)
    own = own_a[SPLIT + 4 : SPLIT + 5, :].astype(jnp.int32)
    far = other_a[SPLIT + 4 : SPLIT + 5, :].astype(jnp.int32)
    low, high = jnp.where(first, own, far), jnp.where(first, far, own)
    text_pos = jnp.concatenate([low[:, 0:256], high[:, 0:256]], axis=1)
    slot_pos = jnp.concatenate([low[:, 256:512], high[:, 256:512] + 4], axis=1)
    rest = text_pos & 15
    block = text_pos >> 4
    place = slot_pos * 128 + ((block & 7) * 2 + (block >> 3)) * 8 + (rest & 7)
    place = jnp.where((rest >> 3) == core, place, -1)

    def slope_copy(block):
        low, high = BLOCK_COLUMNS[block]
        where = (pl.ds(block * 512, 512), pl.ds(low, high - low))
        return pltpu.make_async_copy(slope_ref.at[where], slope_out.at[where], sems.at[block])

    def logits_of(block):
        low, high = BLOCK_COLUMNS[block]
        for w in range(4):
            slot = block * 4 + w
            row = window_ref[slot : slot + 1, :]
            for r in range(0, 128, 32):
                products[slot * 128 + r : slot * 128 + r + 32, :] = (
                    texts[r : r + 32, :] * row
                ).astype(BF16)
        return lax.dot_general(
            products[block * 512 : (block + 1) * 512, :],
            half_ref[low:high, :],
            (((1,), (1,)), ((), ())),
            preferred_element_type=F32,
        )

    def slope_of(block, dots):
        low, high = BLOCK_COLUMNS[block]
        place_here = place[:, low:high] - block * 512
        for r in range(0, 512, 32):
            rows = lax.broadcasted_iota(jnp.int32, (32, high - low), 0) + r
            value = jax.nn.sigmoid(temper * dots[r : r + 32, :] + offset)
            value = temper * jnp.where(rows == place_here, value - 1.0, value)
            slope_ref[block * 512 + r : block * 512 + r + 32, low:high] = value.astype(BF16)
        slope_copy(block).start()

    def grads_of(block):
        low, high = BLOCK_COLUMNS[block]
        slope = slope_ref[block * 512 : (block + 1) * 512, low:high]
        for n in range(0, 1024, 256):
            grads = jnp.dot(slope, half_ref[low:high, n : n + 256], preferred_element_type=F32)
            for c in range(n, n + 256, 128):
                part = None if block == 0 else total[:, c : c + 128]
                text = texts[:, c : c + 128]
                for w in range(4):
                    slot = block * 4 + w
                    grad = grads[w * 128 : (w + 1) * 128, c - n : c - n + 128]
                    more = grad * window_ref[slot : slot + 1, c : c + 128]
                    part = more if part is None else part + more
                    audio_sum[slot : slot + 1, c : c + 128] = jnp.sum(grad * text, axis=0, keepdims=True)
                if block < 3:
                    total[:, c : c + 128] = part
                    continue
                tiles = part.reshape(8, 16, 128)
                top = c // 128 % 2 * 8
                for half in range(2):
                    text_ref[half * 4 + c // 256, :, top : top + 8, :] = tiles[:, half * 8 : half * 8 + 8, :]

    dots = logits_of(0)
    for block in range(4):
        slope_of(block, dots)
        if block < 3:
            dots = logits_of(block + 1)
        grads_of(block)
    for level, (keep_ref, send_ref) in enumerate(((keep_self, send_self), (keep_next, send_next))):
        even = audio_sum[level * 8 : level * 8 + 4, :]
        odd = audio_sum[level * 8 + 4 : level * 8 + 8, :]
        keep_ref[...] = jnp.where(first, even, odd)
        send_ref[...] = jnp.where(first, odd, even)
    for block in range(4):
        slope_copy(block).wait()


def image_kernel(
    core_ref, texts, window_ref, slope_hbm, own_ref, other_a, other_b, products, slope_ref, sems
):
    core = core_ref[0]

    def slope_copy(n):
        where = (pl.ds(n * 512, 1536), pl.ds(n * 256, 256))
        return pltpu.make_async_copy(slope_hbm.at[where], slope_ref.at[where], sems.at[n])

    slope_copy(0).start()
    slope_copy(1).start()
    for slot in range(16):
        products[slot * 128 : (slot + 1) * 128, :] = (
            texts[...] * window_ref[slot : slot + 1, :]
        ).astype(BF16)
    slope_copy(0).wait()
    slope_copy(1).wait()
    grads = [
        lax.dot_general(
            slope_ref[n * 512 : n * 512 + 1536, n * 256 : (n + 1) * 256],
            products[n * 512 : n * 512 + 1536, :],
            (((0,), (0,)), ((), ())),
            preferred_element_type=F32,
        )
        for n in range(2)
    ]
    first = core == 0
    own_ref[...] = jnp.where(first, grads[0], grads[1])
    other_a[...] = jnp.where(first, grads[1][0:128], grads[0][0:128])
    other_b[...] = jnp.where(first, grads[1][128:256], grads[0][128:256])


def second_kernel(parts_ref, own_ref, next_ref, far_ref, came_ref, out_ref):
    total = parts_ref[0]
    for n in range(1, 8):
        total = total + parts_ref[n]
    out_ref[:, 0:16, :] = total
    audio = (own_ref[...] + came_ref[...]) + (next_ref[...] + far_ref[...])
    for c in range(8):
        rows = audio[:, c * 128 : (c + 1) * 128]
        out_ref[:, 16 + c * 4 : 20 + c * 4, :] = jnp.broadcast_to(rows[None], (8, 4, 128))


def third_kernel(parts_ref, audio_ref, piece_ref):
    total = parts_ref[0]
    for n in range(1, 8):
        total = total + parts_ref[n]
    for c in range(8):
        audio_ref[:, c * 128 : (c + 1) * 128] = total[16 + c * 4 : 20 + c * 4, :]
    piece_ref[...] = jnp.broadcast_to(total[0:16, :][None], (32, 16, 128))


def last_kernel(pieces_ref, mine_ref, fixed_ref, out_ref, audio_ref):
    audio_ref[...] = mine_ref[...] + fixed_ref[...]
    for core in range(2):
        for low in range(4):
            total = pieces_ref[low * 2 + core]
            for x in range(1, 4):
                total = total + pieces_ref[(x * 4 + low) * 2 + core]
            for n in range(2):
                left = (low * 2 + n) * 128
                out_ref[core * 8 : core * 8 + 8, left : left + 128] = total[n * 8 : n * 8 + 8, :]


def call(kernel, outs, specs, scratch=(), flops=0, moved=1 << 20, room=4, out_specs=None):
    return pl.pallas_call(
        kernel,
        out_shape=[o if hasattr(o, "shape") else jax.ShapeDtypeStruct(*o) for o in outs],
        in_specs=specs,
        out_specs=out_specs or [VMEM] * len(outs),
        scratch_shapes=list(scratch),
        compiler_params=pltpu.CompilerParams(vmem_limit_bytes=room << 20),
        cost_estimate=pl.CostEstimate(flops=flops, bytes_accessed=moved, transcendentals=0),
    )


def shards(images, texts, audio, pos_text, pos_audio, logit_scale, logit_bias):
    core = (lax.axis_index("aud") % 2).astype(jnp.int32)
    core_arg = core.reshape(1)

    half_block = lax.dynamic_slice_in_dim(texts, core * 8, 8, 0)
    spread = jnp.broadcast_to(half_block[None], (N_TXT, 8, 1024))
    spread, audio = lax.optimization_barrier((spread, audio))
    gathered = lax.all_to_all(spread, BOTH, 0, 0, tiled=True, axis_index_groups=TEXT_GROUPS)
    gathered = gathered.reshape(128, 1024)

    own_a, own_b = call(
        pack_kernel, [((SPLIT + 8, 1024), F32), ((256 - SPLIT, 1024), F32)], [VMEM] * 4
    )(*(pltpu.with_memory_space_constraint(v, pltpu.HBM) for v in (images, audio, pos_text.reshape(1, 256), pos_audio.reshape(1, 256))))
    other_a = lax.ppermute(own_a, "aud", OTHER_CORE)
    other_b = lax.ppermute(own_b, "aud", OTHER_CORE)
    small = pl.BlockSpec((8, 1024), lambda i: (SPLIT // 8, 0))
    pair = pl.pallas_call(
        pair_kernel,
        out_shape=jax.ShapeDtypeStruct((8, 1024), F32),
        grid=(1,),
        in_specs=[small, small],
        out_specs=pl.BlockSpec((8, 1024), lambda i: (0, 0)),
        compiler_params=pltpu.CompilerParams(vmem_limit_bytes=1 << 20),
    )(own_a, other_a)
    next_pair = lax.ppermute(pair, "aud", FROM_NEXT)

    slope, text_parts, keep_self, keep_next, send_self, send_next, window = call(
        slope_kernel,
        [
            pltpu.HBM((2048, 512), BF16),
            ((8, 8, 16, 128), F32),
            ((4, 1024), F32),
            ((4, 1024), F32),
            ((4, 1024), F32),
            ((4, 1024), F32),
            ((16, 1024), F32),
        ],
        [SMEM] * 3 + [VMEM] * 6,
        [
            pltpu.VMEM((512, 1024), BF16),
            pltpu.VMEM((2048, 512), BF16),
            pltpu.VMEM((2048, 1024), BF16),
            pltpu.VMEM((16, 1024), F32),
            pltpu.VMEM((128, 1024), F32),
            pltpu.SemaphoreType.DMA((4,)),
        ],
        flops=3_300_000_000,
        moved=4 << 20,
        room=26,
        out_specs=[pl.BlockSpec(memory_space=pltpu.HBM)] + [VMEM] * 6,
    )(core_arg, logit_scale, logit_bias, gathered, own_a, own_b, other_a, other_b, next_pair)

    parts = lax.all_to_all(text_parts, BOTH, 0, 0, tiled=True, axis_index_groups=Y_GROUPS)

    home = [
        lax.ppermute(keep_next, "aud", TO_NEXT),
        lax.ppermute(send_next, "aud", TO_NEXT_OTHER),
        lax.ppermute(send_self, "aud", OTHER_CORE),
    ]
    window = lax.optimization_barrier((window, home[2]))[0]

    own_grad, *other_grads = call(
        image_kernel,
        [((256, 1024), F32), ((128, 1024), F32), ((128, 1024), F32)],
        [SMEM, VMEM, VMEM, pl.BlockSpec(memory_space=pltpu.HBM)],
        [
            pltpu.VMEM((2048, 1024), BF16),
            pltpu.VMEM((2048, 512), BF16),
            pltpu.SemaphoreType.DMA((2,)),
        ],
        flops=1_700_000_000,
        moved=5 << 20,
        room=24,
    )(core_arg, gathered, window, pltpu.with_memory_space_constraint(slope, pltpu.HBM))
    keep_self, *other_grads = lax.optimization_barrier((keep_self, *other_grads))
    (second,) = call(second_kernel, [((8, 48, 128), F32)], [VMEM] * 5)(parts, keep_self, *home)
    other_grads = lax.optimization_barrier((*other_grads, second))[:2]
    second = lax.all_to_all(second, BOTH, 0, 0, tiled=True, axis_index_groups=Z_GROUPS)
    mine, piece = call(
        third_kernel, [((4, 1024), F32), ((32, 16, 128), F32)], [VMEM]
    )(second)
    pieces = lax.all_to_all(piece, "aud", 0, 0, tiled=True)
    fixed = lax.ppermute(mine, "txt", OTHER_HALF)
    came_grads = [lax.ppermute(grad, "aud", OTHER_CORE) for grad in other_grads]
    grad_images = own_grad + jnp.concatenate(came_grads)
    fixed, grad_images = lax.optimization_barrier((fixed, grad_images))
    grad_texts, grad_audio = call(
        last_kernel, [((16, 1024), F32), ((4, 1024), F32)], [VMEM] * 3
    )(pieces, mine, fixed)
    return (grad_images, grad_texts, grad_audio)


def solution(mesh):
    placed = (
        P(("txt", "aud"), None),
        P("txt", None),
        P("aud", None),
        P(("txt", "aud")),
        P(("txt", "aud")),
        P(),
        P(),
    )
    return jax.shard_map(
        shards,
        mesh=mesh,
        in_specs=placed,
        out_specs=(P(("txt", "aud"), None), P("txt", None), P("aud", None)),
        check_vma=False,
    )
```

```python
import jax
import jax.numpy as jnp
from jax import lax
from jax.experimental import pallas as pl
from jax.experimental.pallas import tpu as pltpu
from jax.sharding import PartitionSpec as P

BOTH = ("txt", "aud")
N_TXT, N_AUD = 16, 32
SPLIT = 128
F32, BF16 = jnp.float32, jnp.bfloat16
VMEM = pl.BlockSpec(memory_space=pltpu.VMEM)
SMEM = pl.BlockSpec(memory_space=pltpu.SMEM)


def device(high, z, x, low, core):
    return (high * 8 + z) * N_AUD + (x * 4 + low) * 2 + core


def groups_by(key):
    found = {}
    for high in range(2):
        for z in range(8):
            for x in range(4):
                for low in range(4):
                    for core in range(2):
                        place = (high, z, x, low, core)
                        found.setdefault(key(*place), []).append(device(*place))
    return [found[k] for k in sorted(found)]


TEXT_GROUPS = [
    [group[p % 2 * 8 + p // 2] for p in range(N_TXT)]
    for group in groups_by(lambda high, z, x, low, core: (x, low if high == 0 else 3 - low, core))
]
Y_GROUPS = groups_by(lambda high, z, x, low, core: (z, x, core))
Z_GROUPS = groups_by(lambda high, z, x, low, core: (high, x, low, core))

OTHER_CORE = [(i, i ^ 1) for i in range(N_AUD)]
FROM_NEXT = [(i, (i - 2) % N_AUD) for i in range(N_AUD)]
OTHER_HALF = [(i, i ^ 8) for i in range(N_TXT)]
TO_NEXT = [(i, (i + 2) % N_AUD) for i in range(N_AUD)]
TO_NEXT_OTHER = [(i, ((i + 2) % N_AUD) ^ 1) for i in range(N_AUD)]


BLOCK_COLUMNS = ((0, 256), (0, 512), (0, 512), (256, 512))


def pack_kernel(images_ref, audio_ref, text_ref, slot_ref, first_ref, rest_ref):
    first_ref[0:SPLIT, :] = images_ref[0:SPLIT, :]
    rest_ref[...] = images_ref[SPLIT:256, :]
    first_ref[SPLIT : SPLIT + 8, :] = jnp.zeros((8, 1024), F32)
    first_ref[SPLIT : SPLIT + 4, :] = audio_ref[...]
    first_ref[SPLIT + 4 : SPLIT + 5, 0:256] = text_ref[...].astype(F32)
    first_ref[SPLIT + 4 : SPLIT + 5, 256:512] = slot_ref[...].astype(F32)


def pair_kernel(own_ref, far_ref, pair_ref):
    pair_ref[0:4, :] = own_ref[0:4, :]
    pair_ref[4:8, :] = far_ref[0:4, :]


def slope_kernel(
    core_ref, scale_ref, bias_ref, texts, own_a, own_b, other_a, other_b, next_pair,
    slope_out, text_ref, keep_self, keep_next, send_self, send_next, window_ref,
    half_ref, slope_ref, products, audio_sum, total, sems,
):
    core = core_ref[0]
    first = core == 0
    temper, offset = scale_ref[0], bias_ref[0]
    for level, (a, b) in enumerate(
        ((own_a[SPLIT : SPLIT + 4, :], other_a[SPLIT : SPLIT + 4, :]), (next_pair[0:4, :], next_pair[4:8, :]))
    ):
        window_ref[level * 8 : level * 8 + 4, :] = jnp.where(first, a, b)
        window_ref[level * 8 + 4 : level * 8 + 8, :] = jnp.where(first, b, a)
    for which, a, b in ((core, own_a, own_b), (1 - core, other_a, other_b)):
        top = pl.multiple_of(which * 256, 256)
        middle = pl.multiple_of(which * 256 + SPLIT, 32)
        half_ref[pl.ds(top, SPLIT), :] = a[0:SPLIT, :].astype(BF16)
        half_ref[pl.ds(middle, 256 - SPLIT), :] = b[...].astype(BF16)
    own = own_a[SPLIT + 4 : SPLIT + 5, :].astype(jnp.int32)
    far = other_a[SPLIT + 4 : SPLIT + 5, :].astype(jnp.int32)
    low, high = jnp.where(first, own, far), jnp.where(first, far, own)
    text_pos = jnp.concatenate([low[:, 0:256], high[:, 0:256]], axis=1)
    slot_pos = jnp.concatenate([low[:, 256:512], high[:, 256:512] + 4], axis=1)
    rest = text_pos & 15
    block = text_pos >> 4
    place = slot_pos * 128 + ((block & 7) * 2 + (block >> 3)) * 8 + (rest & 7)
    place = jnp.where((rest >> 3) == core, place, -1)

    def slope_copy(block):
        low, high = BLOCK_COLUMNS[block]
        where = (pl.ds(block * 512, 512), pl.ds(low, high - low))
        return pltpu.make_async_copy(slope_ref.at[where], slope_out.at[where], sems.at[block])

    def logits_of(block):
        low, high = BLOCK_COLUMNS[block]
        for w in range(4):
            slot = block * 4 + w
            row = window_ref[slot : slot + 1, :]
            for r in range(0, 128, 32):
                products[slot * 128 + r : slot * 128 + r + 32, :] = (
                    texts[r : r + 32, :] * row
                ).astype(BF16)
        return lax.dot_general(
            products[block * 512 : (block + 1) * 512, :],
            half_ref[low:high, :],
            (((1,), (1,)), ((), ())),
            preferred_element_type=F32,
        )

    def slope_of(block, dots):
        low, high = BLOCK_COLUMNS[block]
        place_here = place[:, low:high] - block * 512
        for r in range(0, 512, 32):
            rows = lax.broadcasted_iota(jnp.int32, (32, high - low), 0) + r
            value = jax.nn.sigmoid(temper * dots[r : r + 32, :] + offset)
            value = temper * jnp.where(rows == place_here, value - 1.0, value)
            slope_ref[block * 512 + r : block * 512 + r + 32, low:high] = value.astype(BF16)
        slope_copy(block).start()

    def grads_of(block):
        low, high = BLOCK_COLUMNS[block]
        slope = slope_ref[block * 512 : (block + 1) * 512, low:high]
        for n in range(0, 1024, 256):
            grads = jnp.dot(slope, half_ref[low:high, n : n + 256], preferred_element_type=F32)
            for c in range(n, n + 256, 128):
                part = None if block == 0 else total[:, c : c + 128]
                text = texts[:, c : c + 128]
                for w in range(4):
                    slot = block * 4 + w
                    grad = grads[w * 128 : (w + 1) * 128, c - n : c - n + 128]
                    more = grad * window_ref[slot : slot + 1, c : c + 128]
                    part = more if part is None else part + more
                    audio_sum[slot : slot + 1, c : c + 128] = jnp.sum(grad * text, axis=0, keepdims=True)
                if block < 3:
                    total[:, c : c + 128] = part
                    continue
                tiles = part.reshape(8, 16, 128)
                top = c // 128 % 2 * 8
                for half in range(2):
                    text_ref[half * 4 + c // 256, :, top : top + 8, :] = tiles[:, half * 8 : half * 8 + 8, :]

    dots = logits_of(0)
    for block in range(4):
        slope_of(block, dots)
        if block < 3:
            dots = logits_of(block + 1)
        grads_of(block)
    for level, (keep_ref, send_ref) in enumerate(((keep_self, send_self), (keep_next, send_next))):
        even = audio_sum[level * 8 : level * 8 + 4, :]
        odd = audio_sum[level * 8 + 4 : level * 8 + 8, :]
        keep_ref[...] = jnp.where(first, even, odd)
        send_ref[...] = jnp.where(first, odd, even)
    for block in range(4):
        slope_copy(block).wait()


def image_kernel(
    core_ref, texts, window_ref, slope_hbm, own_ref, other_a, other_b, products, slope_ref, sems
):
    core = core_ref[0]

    def slope_copy(n):
        where = (pl.ds(n * 512, 1536), pl.ds(n * 256, 256))
        return pltpu.make_async_copy(slope_hbm.at[where], slope_ref.at[where], sems.at[n])

    slope_copy(0).start()
    slope_copy(1).start()
    for slot in range(16):
        products[slot * 128 : (slot + 1) * 128, :] = (
            texts[...] * window_ref[slot : slot + 1, :]
        ).astype(BF16)
    slope_copy(0).wait()
    slope_copy(1).wait()
    grads = [
        lax.dot_general(
            slope_ref[n * 512 : n * 512 + 1536, n * 256 : (n + 1) * 256],
            products[n * 512 : n * 512 + 1536, :],
            (((0,), (0,)), ((), ())),
            preferred_element_type=F32,
        )
        for n in range(2)
    ]
    first = core == 0
    own_ref[...] = jnp.where(first, grads[0], grads[1])
    other_a[...] = jnp.where(first, grads[1][0:128], grads[0][0:128])
    other_b[...] = jnp.where(first, grads[1][128:256], grads[0][128:256])


def second_kernel(parts_ref, own_ref, next_ref, far_ref, came_ref, out_ref):
    total = parts_ref[0]
    for n in range(1, 8):
        total = total + parts_ref[n]
    out_ref[:, 0:16, :] = total
    audio = (own_ref[...] + came_ref[...]) + (next_ref[...] + far_ref[...])
    for c in range(8):
        rows = audio[:, c * 128 : (c + 1) * 128]
        out_ref[:, 16 + c * 4 : 20 + c * 4, :] = jnp.broadcast_to(rows[None], (8, 4, 128))


def third_kernel(parts_ref, audio_ref, piece_ref):
    total = parts_ref[0]
    for n in range(1, 8):
        total = total + parts_ref[n]
    for c in range(8):
        audio_ref[:, c * 128 : (c + 1) * 128] = total[16 + c * 4 : 20 + c * 4, :]
    piece_ref[...] = jnp.broadcast_to(total[0:16, :][None], (32, 16, 128))


def last_kernel(pieces_ref, mine_ref, fixed_ref, out_ref, audio_ref):
    audio_ref[...] = mine_ref[...] + fixed_ref[...]
    for core in range(2):
        for low in range(4):
            total = pieces_ref[low * 2 + core]
            for x in range(1, 4):
                total = total + pieces_ref[(x * 4 + low) * 2 + core]
            for n in range(2):
                left = (low * 2 + n) * 128
                out_ref[core * 8 : core * 8 + 8, left : left + 128] = total[n * 8 : n * 8 + 8, :]


def call(kernel, outs, specs, scratch=(), flops=0, moved=1 << 20, room=4, out_specs=None):
    return pl.pallas_call(
        kernel,
        out_shape=[o if hasattr(o, "shape") else jax.ShapeDtypeStruct(*o) for o in outs],
        in_specs=specs,
        out_specs=out_specs or [VMEM] * len(outs),
        scratch_shapes=list(scratch),
        compiler_params=pltpu.CompilerParams(vmem_limit_bytes=room << 20),
        cost_estimate=pl.CostEstimate(flops=flops, bytes_accessed=moved, transcendentals=0),
    )


def shards(images, texts, audio, pos_text, pos_audio, logit_scale, logit_bias):
    core = (lax.axis_index("aud") % 2).astype(jnp.int32)
    core_arg = core.reshape(1)

    half_block = lax.dynamic_slice_in_dim(texts, core * 8, 8, 0)
    spread = jnp.broadcast_to(half_block[None], (N_TXT, 8, 1024))
    spread, audio = lax.optimization_barrier((spread, audio))
    gathered = lax.all_to_all(spread, BOTH, 0, 0, tiled=True, axis_index_groups=TEXT_GROUPS)
    gathered = gathered.reshape(128, 1024)

    own_a, own_b = call(
        pack_kernel, [((SPLIT + 8, 1024), F32), ((256 - SPLIT, 1024), F32)], [VMEM] * 4
    )(*(pltpu.with_memory_space_constraint(v, pltpu.HBM) for v in (images, audio, pos_text.reshape(1, 256), pos_audio.reshape(1, 256))))
    other_a = lax.ppermute(own_a, "aud", OTHER_CORE)
    other_b = lax.ppermute(own_b, "aud", OTHER_CORE)
    small = pl.BlockSpec((8, 1024), lambda i: (SPLIT // 8, 0))
    pair = pl.pallas_call(
        pair_kernel,
        out_shape=jax.ShapeDtypeStruct((8, 1024), F32),
        grid=(1,),
        in_specs=[small, small],
        out_specs=pl.BlockSpec((8, 1024), lambda i: (0, 0)),
        compiler_params=pltpu.CompilerParams(vmem_limit_bytes=1 << 20),
    )(own_a, other_a)
    next_pair = lax.ppermute(pair, "aud", FROM_NEXT)

    slope, text_parts, keep_self, keep_next, send_self, send_next, window = call(
        slope_kernel,
        [
            pltpu.HBM((2048, 512), BF16),
            ((8, 8, 16, 128), F32),
            ((4, 1024), F32),
            ((4, 1024), F32),
            ((4, 1024), F32),
            ((4, 1024), F32),
            ((16, 1024), F32),
        ],
        [SMEM] * 3 + [VMEM] * 6,
        [
            pltpu.VMEM((512, 1024), BF16),
            pltpu.VMEM((2048, 512), BF16),
            pltpu.VMEM((2048, 1024), BF16),
            pltpu.VMEM((16, 1024), F32),
            pltpu.VMEM((128, 1024), F32),
            pltpu.SemaphoreType.DMA((4,)),
        ],
        flops=3_300_000_000,
        moved=4 << 20,
        room=26,
        out_specs=[pl.BlockSpec(memory_space=pltpu.HBM)] + [VMEM] * 6,
    )(core_arg, logit_scale, logit_bias, gathered, own_a, own_b, other_a, other_b, next_pair)

    parts = lax.all_to_all(text_parts, BOTH, 0, 0, tiled=True, axis_index_groups=Y_GROUPS)

    home = [
        lax.ppermute(keep_next, "aud", TO_NEXT),
        lax.ppermute(send_next, "aud", TO_NEXT_OTHER),
        lax.ppermute(send_self, "aud", OTHER_CORE),
    ]

    own_grad, *other_grads = call(
        image_kernel,
        [((256, 1024), F32), ((128, 1024), F32), ((128, 1024), F32)],
        [SMEM, VMEM, VMEM, pl.BlockSpec(memory_space=pltpu.HBM)],
        [
            pltpu.VMEM((2048, 1024), BF16),
            pltpu.VMEM((2048, 512), BF16),
            pltpu.SemaphoreType.DMA((2,)),
        ],
        flops=1_700_000_000,
        moved=5 << 20,
        room=24,
    )(core_arg, gathered, window, pltpu.with_memory_space_constraint(slope, pltpu.HBM))
    keep_self, *other_grads = lax.optimization_barrier((keep_self, *other_grads))
    (second,) = call(second_kernel, [((8, 48, 128), F32)], [VMEM] * 5)(parts, keep_self, *home)
    other_grads = lax.optimization_barrier((*other_grads, second))[:2]
    second = lax.all_to_all(second, BOTH, 0, 0, tiled=True, axis_index_groups=Z_GROUPS)
    mine, piece = call(
        third_kernel, [((4, 1024), F32), ((32, 16, 128), F32)], [VMEM]
    )(second)
    pieces = lax.all_to_all(piece, "aud", 0, 0, tiled=True)
    fixed = lax.ppermute(mine, "txt", OTHER_HALF)
    came_grads = [lax.ppermute(grad, "aud", OTHER_CORE) for grad in other_grads]
    grad_images = own_grad + jnp.concatenate(came_grads)
    fixed, grad_images = lax.optimization_barrier((fixed, grad_images))
    grad_texts, grad_audio = call(
        last_kernel, [((16, 1024), F32), ((4, 1024), F32)], [VMEM] * 3
    )(pieces, mine, fixed)
    return (grad_images, grad_texts, grad_audio)


def solution(mesh):
    placed = (
        P(("txt", "aud"), None),
        P("txt", None),
        P("aud", None),
        P(("txt", "aud")),
        P(("txt", "aud")),
        P(),
        P(),
    )
    return jax.shard_map(
        shards,
        mesh=mesh,
        in_specs=placed,
        out_specs=(P(("txt", "aud"), None), P("txt", None), P("aud", None)),
        check_vma=False,
    )
```
